32 devices in a mesh: groups: 2 (over x), section: 2 (over core), tensor: 8 (over z, y).
Axes of the slice: x: 2, y: 2, z: 4, core: 2. Of those that a mesh axis runs over, the one named last changes fastest.
Arguments:
- hidden: bfloat16 [2, 1024, 26624], P('section', 'groups', 'tensor'), parts along dimension 1, may hold values from -6 to 6
- down_weight: bfloat16 [2, 26624, 8192], P('section', 'tensor'), may hold values from -0.0546875 to 0.0546875
- residual: bfloat16 [2, 1024, 8192], P('section', 'groups', 'tensor'), parts along dimension 1, may hold values from -100 to 100
- norm_gain: float32 [2, 8192], P('section'), may hold values from 0.1 to 1.9
- qkv_weight: bfloat16 [2, 8192, 9216], P('section', None, 'tensor'), may hold values from -0.0625 to 0.0625
Outputs:
- received: bfloat16 [2, 1024, 8192], P('section', 'groups', 'tensor'), parts along dimension 1
- projected: bfloat16 [2, 1024, 9216], P('section', 'groups', 'tensor'), parts along dimension 1
The draws below stay inside these ranges and needn't reach their ends.
There are 2 independent parts, one for each index of `groups`. The reference program is written for one: setup_inputs(seed, part) draws one part's arguments, and reference() takes and returns one part's arrays. A program takes and returns all parts, laid end to end along the dimension named above; an argument that names none is the same for every part. Nothing has to cross between parts.
All inputs are finite; a program needn't handle non-finite values.
Results may differ from the reference program's by a relative error of at most 0.0057.
Values may be sent and summed in bfloat16 or wider, within the bound.
A program may use at most 192 MiB of HBM per device.

```python
import jax
import jax.numpy as jnp
from jax import lax

D = 8192
FF = 26624
TOK = 512
QKV = 9216
SECTIONS = 2


def draw_residual(key, part):
    key_base = jax.random.fold_in(key, 11)
    key_rows = jax.random.fold_in(key, 12)
    key_cols = jax.random.fold_in(key, 13)
    ramp = 10.0 ** (jnp.arange(D, dtype=jnp.float32) / D - 0.5)
    rough = jax.random.uniform(key_cols, (D,), jnp.float32, 0.5, 1.5)
    base = jax.random.truncated_normal(key_base, -6.0, 6.0, (SECTIONS, TOK, D), jnp.float32)
    rows = 10.0 ** jax.random.uniform(key_rows, (SECTIONS, TOK, 1), jnp.float32, -0.5, 0.5)
    return (base * rows * ramp[None, None, :] * rough[None, None, :]).astype(jnp.bfloat16)


def with_spikes(entries, rng, source, target, parts, factor):
    owner, partner = [(jnp.arange(entries.shape[dim]) // (entries.shape[dim] // parts)).reshape([-1 if axis == dim else 1 for axis in range(entries.ndim)]) for dim in (source, target)]
    chosen = jax.random.permutation(rng, parts)[partner]
    strong = (owner == chosen) | (owner == (partner + parts // 2) % parts)
    return jnp.where(strong, factor * entries, entries)


def levels(stream_key, extent, split, least, high):
    level, own = 1.0, jax.random.fold_in(stream_key, 6)
    for position, blocks in split:
        steps = jnp.exp(jax.random.uniform(jax.random.fold_in(own, position), (blocks,), jnp.float32, least / len(split), high / len(split)))
        level = level * jnp.repeat(steps, extent[position] // blocks).reshape([-1 if axis == position else 1 for axis in range(len(extent))])
    return level


def gaussian(key, extent, spread, reach, cuts=(), held_as=jnp.bfloat16):
    array = spread * jax.random.normal(key, extent, jnp.float32)
    if cuts:
        array = array * levels(key, extent, cuts, -0.22, 0.18)
    return jnp.clip(array, -reach, reach).astype(held_as)


def bell_draw_with(own_key, dims, deviation, bound, split, heavy, kind=jnp.bfloat16):
    array = deviation * jax.random.normal(own_key, dims, jnp.float32)
    if split:
        array = array * levels(own_key, dims, split, -0.22, 0.18)
    return jnp.clip(with_spikes(array, jax.random.fold_in(own_key, 3), *heavy), -bound, bound).astype(kind)


def setup_inputs(seed: int = 0, part: int = 0) -> dict:
    arg_keys = jax.random.split(jax.random.key(seed), 6)
    own_keys = jax.random.split(jax.random.fold_in(arg_keys[5], part), 6)
    return {
        "hidden": gaussian(own_keys[0], (SECTIONS, TOK, FF), 1.0, 6.0, ((0, 2), (2, 8))),
        "down_weight": bell_draw_with(arg_keys[1], (SECTIONS, FF, D), FF ** -0.5, 0.0546875, ((0, 2), (1, 8)), (1, 2, 8, 2.0)),
        "residual": draw_residual(jax.random.fold_in(jax.random.fold_in(arg_keys[5], part), 71), part),
        "norm_gain": jnp.clip(1.0 + 0.18 * jax.random.normal(arg_keys[3], (SECTIONS, D), jnp.float32), 0.1, 1.9),
        "qkv_weight": gaussian(arg_keys[4], (SECTIONS, D, QKV), D ** -0.5, 0.0625, ((0, 2), (2, 8))),
    }


epsilon = 1e-05

def reference(hidden, down_weight, residual, norm_gain, qkv_weight):
    streams = []
    for section_idx in range(SECTIONS):
        partial_sum = jnp.dot(hidden[section_idx], down_weight[section_idx], preferred_element_type=jnp.float32)
        streams.append((residual[section_idx].astype(jnp.float32) + partial_sum).astype(jnp.bfloat16))
    stream = jnp.stack(streams)
    received = jnp.roll(stream, 1, axis=0)
    outputs = []
    for section_idx in range(SECTIONS):
        floats = received[section_idx].astype(jnp.float32)
        square_sum = lax.optimization_barrier(jnp.sum(floats * floats, axis=1, keepdims=True))
        scale_inv = lax.rsqrt(square_sum / D + epsilon)
        normed = (floats * scale_inv * norm_gain[section_idx][None, :]).astype(jnp.bfloat16)
        outputs.append(jnp.dot(normed, qkv_weight[section_idx], preferred_element_type=jnp.float32).astype(jnp.bfloat16))
    return (received, jnp.stack(outputs))
```

```python
import functools

import jax
import jax.numpy as jnp
from jax import lax
from jax.experimental import pallas as pl
from jax.experimental.pallas import tpu as pltpu
from jax.sharding import PartitionSpec as P

epsilon = 1e-05
MESH = pl.DeviceIdType.MESH
PIECES = 2
BUFFERS = 4


def ring_order(n):
    inner = 1
    while inner * inner * 4 <= n:
        inner *= 2
    outer = n // inner
    if outer * inner != n or inner < 2 or outer % 2:
        return list(range(n))
    order = []
    for a in range(outer):
        columns = range(1, inner) if a % 2 == 0 else range(inner - 1, 0, -1)
        order += [a * inner + b for b in columns]
    return order + [a * inner for a in range(outer - 1, -1, -1)]


def lookup(table, index):
    found = jnp.int32(table[0])
    for k in range(1, len(table)):
        found = jnp.where(index == k, jnp.int32(table[k]), found)
    return found


def kernel(n, sections, hidden, down, residual, gain, qkv, received, projected,
           w_buf, q_buf, part, rs, ag, acc, square, w_sem, q_sem, rs_send, rs_recv,
           ag_send, ag_recv, swap_send, swap_recv):
    order = ring_order(n)
    position = [order.index(k) for k in range(n)]
    half, chunk = part.shape[1:]
    width = w_buf.shape[2]
    tiles = chunk // width
    rows = half // PIECES
    total_tiles = n * 2 * tiles

    me = lax.axis_index("tensor")
    here = lookup(position, me)
    at = lambda p: lookup(order, lax.rem(p + 2 * n, n))
    right, left = at(here + 1), at(here - 1)
    section = lax.axis_index("section")
    after = lax.rem(section + 1, sections)
    before = lax.rem(section + sections - 1, sections)
    towards = (right, left)

    def owner(s, d):
        return at(here - s) if d == 0 else at(here + s)

    def fetch(t):
        s = lax.div(t, 2 * tiles)
        d = lax.rem(lax.div(t, tiles), 2)
        j = lax.rem(t, tiles)
        c = at(here + (2 * d - 1) * (s + 1))
        start = pl.multiple_of(c * chunk + j * width, width)
        b = lax.rem(t, BUFFERS)
        return pltpu.make_async_copy(down.at[:, pl.ds(start, width)], w_buf.at[b], w_sem.at[b])

    for t in range(min(BUFFERS, total_tiles)):
        fetch(jnp.int32(t)).start()

    barrier = pltpu.get_barrier_semaphore()
    pl.semaphore_signal(barrier, inc=1, device_id={"tensor": left}, device_id_type=MESH)
    pl.semaphore_signal(barrier, inc=1, device_id={"tensor": right}, device_id_type=MESH)
    pl.semaphore_signal(barrier, inc=1, device_id={"section": before}, device_id_type=MESH)
    pl.semaphore_wait(barrier, 3)

    def span(piece):
        return pl.ds(piece * rows, rows)

    def rs_copy(s, d, piece):
        return pltpu.make_async_remote_copy(
            src_ref=rs.at[s, d, span(piece)],
            dst_ref=rs.at[s + 1, d, span(piece)],
            send_sem=rs_send.at[d, piece, lax.rem(s, 2)],
            recv_sem=rs_recv.at[d, piece, s],
            device_id={"tensor": towards[d]}, device_id_type=MESH)

    def swap_copy(d, piece):
        return pltpu.make_async_remote_copy(
            src_ref=rs.at[n - 1, d, span(piece)],
            dst_ref=ag.at[me, d, span(piece)],
            send_sem=swap_send.at[d, piece],
            recv_sem=swap_recv.at[d, piece],
            device_id={"section": after}, device_id_type=MESH)

    def ag_copy(s, d, piece, slot):
        return pltpu.make_async_remote_copy(
            src_ref=ag.at[slot, d, span(piece)],
            dst_ref=ag.at[slot, d, span(piece)],
            send_sem=ag_send.at[d, piece, lax.rem(s, 2)],
            recv_sem=ag_recv.at[d, piece, s],
            device_id={"tensor": towards[d]}, device_id_type=MESH)

    def reduce_step(s, first, last):
        for d in range(2):
            def tile(j, carry):
                t = (s * 2 + d) * tiles + j
                fetch(t).wait()
                part[d, :, pl.ds(pl.multiple_of(j * width, width), width)] = jnp.dot(
                    hidden[pl.ds(d * half, half), :], w_buf[lax.rem(t, BUFFERS)],
                    preferred_element_type=jnp.float32)

                @pl.when(t + BUFFERS < total_tiles)
                def _():
                    fetch(t + BUFFERS).start()
                return carry
            lax.fori_loop(0, tiles, tile, 0)
        for piece in range(PIECES):
            for d in range(2):
                value = part[d, span(piece), :]
                if not first:
                    rs_copy(s - 1, d, piece).wait_recv()
                    value = value + rs[s, d, span(piece), :].astype(jnp.float32)
                if last:
                    value = value + residual[pl.ds(d * half + piece * rows, rows), :].astype(jnp.float32)
                rs[s, d, span(piece), :] = value.astype(jnp.bfloat16)
                if last:
                    swap_copy(d, piece).start()
                else:
                    @pl.when(s >= 2)
                    def _():
                        rs_copy(s - 2, d, piece).wait_send()
                    rs_copy(s, d, piece).start()

    reduce_step(jnp.int32(0), True, False)
    q_copy = pltpu.make_async_copy(qkv, q_buf, q_sem)
    q_copy.start()

    def middle(s, carry):
        reduce_step(s, False, False)
        return carry
    lax.fori_loop(1, n - 1, middle, 0)
    reduce_step(jnp.int32(n - 1), False, True)

    for piece in range(PIECES):
        for d in range(2):
            swap_copy(d, piece).wait_recv()
            ag_copy(jnp.int32(0), d, piece, me).start()
    q_copy.wait()

    def project(d, c, first):
        x = ag[c, d].astype(jnp.float32)
        own = jnp.sum(x * x, axis=1, keepdims=True)
        scaled = (x * gain[c]).astype(jnp.bfloat16)
        product = jnp.dot(scaled, q_buf[c], preferred_element_type=jnp.float32)
        if first:
            square[d] = own
            acc[d] = product
        else:
            square[d] += own
            acc[d] += product

    for d in range(2):
        received[pl.ds(d * half, half), :] = ag[me, d]
        project(d, me, True)

    def gather_step(s, last):
        for piece in range(PIECES):
            for d in range(2):
                slot = owner(s + 1, d)
                ag_copy(s, d, piece, slot).wait_recv()
                if not last:
                    @pl.when(s >= 1)
                    def _():
                        ag_copy(s - 1, d, piece, owner(s - 1, d)).wait_send()
                    ag_copy(s + 1, d, piece, slot).start()
        for d in range(2):
            project(d, owner(s + 1, d), False)

    def gather(s, carry):
        gather_step(s, False)
        return carry
    lax.fori_loop(0, n - 2, gather, 0)
    gather_step(jnp.int32(n - 2), True)

    for d in range(2):
        scale = lax.rsqrt(square[d] / (n * chunk) + epsilon)
        projected[pl.ds(d * half, half), :] = (acc[d] * scale).astype(jnp.bfloat16)

    for piece in range(PIECES):
        for d in range(2):
            swap_copy(d, piece).wait_send()
            for s in range(max(n - 3, 0), n - 1):
                rs_copy(jnp.int32(s), d, piece).wait_send()
                ag_copy(jnp.int32(s), d, piece, owner(s, d)).wait_send()


def body(n, sections, hidden, down_weight, residual, norm_gain, qkv_weight):
    tokens, units = hidden.shape[1:]
    chunk = residual.shape[2]
    columns = qkv_weight.shape[2]
    half = tokens // 2
    width = 256 if chunk % 256 == 0 else chunk
    bf16, f32 = jnp.bfloat16, jnp.float32
    vmem = pl.BlockSpec(memory_space=pltpu.VMEM)
    far = pl.BlockSpec(memory_space=pl.ANY)
    dma = pltpu.SemaphoreType.DMA
    features = n * chunk
    received, projected = pl.pallas_call(
        functools.partial(kernel, n, sections),
        out_shape=(jax.ShapeDtypeStruct((tokens, chunk), bf16),
                   jax.ShapeDtypeStruct((tokens, columns), bf16)),
        in_specs=[vmem, far, vmem, vmem, far],
        out_specs=(vmem, vmem),
        scratch_shapes=[
            pltpu.VMEM((BUFFERS, units, width), bf16),
            pltpu.VMEM((n, chunk, columns), bf16),
            pltpu.VMEM((2, half, chunk), f32),
            pltpu.VMEM((n, 2, half, chunk), bf16),
            pltpu.VMEM((n, 2, half, chunk), bf16),
            pltpu.VMEM((2, half, columns), f32),
            pltpu.VMEM((2, half, 1), f32),
            dma((BUFFERS,)), dma,
            dma((2, PIECES, 2)), dma((2, PIECES, n)),
            dma((2, PIECES, 2)), dma((2, PIECES, n)),
            dma((2, PIECES)), dma((2, PIECES)),
        ],
        compiler_params=pltpu.CompilerParams(
            collective_id=0, has_side_effects=True, vmem_limit_bytes=60 * 2 ** 20),
        cost_estimate=pl.CostEstimate(
            flops=2 * tokens * features * (units + columns),
            bytes_accessed=2 * features * (units + columns), transcendentals=0),
    )(hidden[0], down_weight[0], residual[0],
      norm_gain[0].reshape(n, 1, chunk), qkv_weight[0].reshape(n, chunk, columns))
    return (received[None], projected[None])


def solution(mesh):
    placed = (
        P("section", "groups", "tensor"),
        P("section", "tensor", None),
        P("section", "groups", "tensor"),
        P("section", None),
        P("section", None, "tensor"),
    )
    return jax.shard_map(
        functools.partial(body, mesh.shape["tensor"], mesh.shape["section"]),
        mesh=mesh,
        in_specs=placed,
        out_specs=(P("section", "groups", "tensor"), P("section", "groups", "tensor")),
        check_vma=False,
    )
```

```python
import functools

import jax
import jax.numpy as jnp
from jax import lax
from jax.experimental import pallas as pl
from jax.experimental.pallas import tpu as pltpu
from jax.sharding import PartitionSpec as P

epsilon = 1e-05
MESH = pl.DeviceIdType.MESH
PIECES = 4
BUFFERS = 4


def ring_order(n):
    inner = 1
    while inner * inner * 4 <= n:
        inner *= 2
    outer = n // inner
    if outer * inner != n or inner < 2 or outer % 2:
        return list(range(n))
    order = []
    for a in range(outer):
        columns = range(1, inner) if a % 2 == 0 else range(inner - 1, 0, -1)
        order += [a * inner + b for b in columns]
    return order + [a * inner for a in range(outer - 1, -1, -1)]


def lookup(table, index):
    found = jnp.int32(table[0])
    for k in range(1, len(table)):
        found = jnp.where(index == k, jnp.int32(table[k]), found)
    return found


def kernel(n, sections, hidden, down, residual, gain, qkv, received, projected,
           w_buf, q_buf, part, rs, ag, acc, square, w_sem, q_sem, rs_send, rs_recv,
           ag_send, ag_recv, swap_send, swap_recv):
    order = ring_order(n)
    position = [order.index(k) for k in range(n)]
    half, chunk = part.shape[2:]
    width = w_buf.shape[2]
    tiles = chunk // width
    rows = half // PIECES
    total_tiles = n * 2 * tiles

    me = lax.axis_index("tensor")
    here = lookup(position, me)
    at = lambda p: lookup(order, lax.rem(p + 2 * n, n))
    right, left = at(here + 1), at(here - 1)
    section = lax.axis_index("section")
    after = lax.rem(section + 1, sections)
    before = lax.rem(section + sections - 1, sections)
    towards = (right, left)

    def owner(s, d):
        return at(here - s) if d == 0 else at(here + s)

    def fetch(t):
        s = lax.div(t, 2 * tiles)
        d = lax.rem(lax.div(t, tiles), 2)
        j = lax.rem(t, tiles)
        c = at(here + (2 * d - 1) * (s + 1))
        start = pl.multiple_of(c * chunk + j * width, width)
        b = lax.rem(t, BUFFERS)
        return pltpu.make_async_copy(down.at[:, pl.ds(start, width)], w_buf.at[b], w_sem.at[b])

    for t in range(min(BUFFERS, total_tiles)):
        fetch(jnp.int32(t)).start()

    barrier = pltpu.get_barrier_semaphore()
    pl.semaphore_signal(barrier, inc=1, device_id={"tensor": left}, device_id_type=MESH)
    pl.semaphore_signal(barrier, inc=1, device_id={"tensor": right}, device_id_type=MESH)
    pl.semaphore_signal(barrier, inc=1, device_id={"section": before}, device_id_type=MESH)
    pl.semaphore_wait(barrier, 3)

    def span(piece):
        return pl.ds(piece * rows, rows)

    def rs_copy(s, d, piece):
        return pltpu.make_async_remote_copy(
            src_ref=rs.at[s, d, span(piece)],
            dst_ref=rs.at[s + 1, d, span(piece)],
            send_sem=rs_send.at[d, piece, lax.rem(s, 2)],
            recv_sem=rs_recv.at[d, piece, s],
            device_id={"tensor": towards[d]}, device_id_type=MESH)

    def swap_copy(d, piece):
        return pltpu.make_async_remote_copy(
            src_ref=rs.at[n - 1, d, span(piece)],
            dst_ref=ag.at[me, d, span(piece)],
            send_sem=swap_send.at[d, piece],
            recv_sem=swap_recv.at[d, piece],
            device_id={"section": after}, device_id_type=MESH)

    def ag_copy(s, d, piece, slot):
        return pltpu.make_async_remote_copy(
            src_ref=ag.at[slot, d, span(piece)],
            dst_ref=ag.at[slot, d, span(piece)],
            send_sem=ag_send.at[d, piece, lax.rem(s, 2)],
            recv_sem=ag_recv.at[d, piece, s],
            device_id={"tensor": towards[d]}, device_id_type=MESH)

    def multiply_some(s, first, last):
        def one(i, carry):
            d = lax.div(i, tiles)
            j = lax.rem(i, tiles)
            t = s * 2 * tiles + i
            fetch(t).wait()
            part[lax.rem(s, 2), d, :, pl.ds(pl.multiple_of(j * width, width), width)] = jnp.dot(
                hidden[pl.ds(pl.multiple_of(d * half, half), half), :], w_buf[lax.rem(t, BUFFERS)],
                preferred_element_type=jnp.float32)

            @pl.when(t + BUFFERS < total_tiles)
            def _():
                fetch(t + BUFFERS).start()
            return carry
        lax.fori_loop(first, last, one, 0)

    def combine(s, d, piece, first, last):
        value = part[lax.rem(s, 2), d, span(piece), :]
        if not first:
            rs_copy(s - 1, d, piece).wait_recv()
            value = value + rs[s, d, span(piece), :].astype(jnp.float32)
        if last:
            value = value + residual[pl.ds(d * half + piece * rows, rows), :].astype(jnp.float32)
        rs[s, d, span(piece), :] = value.astype(jnp.bfloat16)
        if last:
            swap_copy(d, piece).start()
        else:
            @pl.when(s >= 2)
            def _():
                rs_copy(s - 2, d, piece).wait_send()
            rs_copy(s, d, piece).start()

    zero = jnp.int32(0)
    for d in range(2):
        multiply_some(zero, d * tiles, (d + 1) * tiles)
        for piece in range(PIECES):
            combine(zero, d, piece, True, False)
    q_copy = pltpu.make_async_copy(qkv, q_buf, q_sem)
    q_copy.start()
    multiply_some(zero + 1, 0, 2 * tiles)

    def middle(s, carry):
        for piece in range(PIECES):
            for d in range(2):
                combine(s, d, piece, False, False)
            multiply_some(s + 1, 2 * tiles * piece // PIECES, 2 * tiles * (piece + 1) // PIECES)
        return carry
    lax.fori_loop(1, n - 1, middle, 0)

    def begin_gather(piece):
        for d in range(2):
            swap_copy(d, piece).wait_recv()
            ag_copy(zero, d, piece, me).start()

    for piece in range(PIECES):
        for d in range(2):
            combine(zero + n - 1, d, piece, False, True)
        if piece:
            begin_gather(piece - 1)
    begin_gather(PIECES - 1)
    q_copy.wait()

    def project(d, c, first):
        x = ag[c, d].astype(jnp.float32)
        own = jnp.sum(x * x, axis=1, keepdims=True)
        scaled = (x * gain[c]).astype(jnp.bfloat16)
        product = jnp.dot(scaled, q_buf[c], preferred_element_type=jnp.float32)
        if first:
            square[d] = own
            acc[d] = product
        else:
            square[d] += own
            acc[d] += product

    for d in range(2):
        received[pl.ds(d * half, half), :] = ag[me, d]
        project(d, me, True)

    def gather_step(s, first, last):
        for piece in range(PIECES):
            for d in range(2):
                slot = owner(s + 1, d)
                ag_copy(s, d, piece, slot).wait_recv()
                if not last:
                    if not first:
                        ag_copy(s - 1, d, piece, owner(s - 1, d)).wait_send()
                    ag_copy(s + 1, d, piece, slot).start()
            if not first and piece in (0, PIECES // 2):
                project(min(piece, 1), owner(s, min(piece, 1)), False)

    gather_step(zero, True, False)

    def gather(s, carry):
        gather_step(s, False, False)
        return carry
    lax.fori_loop(1, n - 2, gather, 0)
    gather_step(zero + n - 2, False, True)
    for d in range(2):
        project(d, owner(n - 1, d), False)

    for d in range(2):
        scale = lax.rsqrt(square[d] / (n * chunk) + epsilon)
        projected[pl.ds(d * half, half), :] = (acc[d] * scale).astype(jnp.bfloat16)

    for piece in range(PIECES):
        for d in range(2):
            swap_copy(d, piece).wait_send()
            for s in range(max(n - 3, 0), n - 1):
                rs_copy(jnp.int32(s), d, piece).wait_send()
                ag_copy(jnp.int32(s), d, piece, owner(s, d)).wait_send()


def body(n, sections, hidden, down_weight, residual, norm_gain, qkv_weight):
    tokens, units = hidden.shape[1:]
    chunk = residual.shape[2]
    columns = qkv_weight.shape[2]
    half = tokens // 2
    width = 256 if chunk % 256 == 0 else chunk
    bf16, f32 = jnp.bfloat16, jnp.float32
    vmem = pl.BlockSpec(memory_space=pltpu.VMEM)
    far = pl.BlockSpec(memory_space=pl.ANY)
    dma = pltpu.SemaphoreType.DMA
    features = n * chunk
    received, projected = pl.pallas_call(
        functools.partial(kernel, n, sections),
        out_shape=(jax.ShapeDtypeStruct((tokens, chunk), bf16),
                   jax.ShapeDtypeStruct((tokens, columns), bf16)),
        in_specs=[vmem, far, vmem, vmem, far],
        out_specs=(vmem, vmem),
        scratch_shapes=[
            pltpu.VMEM((BUFFERS, units, width), bf16),
            pltpu.VMEM((n, chunk, columns), bf16),
            pltpu.VMEM((2, 2, half, chunk), f32),
            pltpu.VMEM((n, 2, half, chunk), bf16),
            pltpu.VMEM((n, 2, half, chunk), bf16),
            pltpu.VMEM((2, half, columns), f32),
            pltpu.VMEM((2, half, 1), f32),
            dma((BUFFERS,)), dma,
            dma((2, PIECES, 2)), dma((2, PIECES, n)),
            dma((2, PIECES, 2)), dma((2, PIECES, n)),
            dma((2, PIECES)), dma((2, PIECES)),
        ],
        compiler_params=pltpu.CompilerParams(
            collective_id=0, has_side_effects=True, vmem_limit_bytes=60 * 2 ** 20),
        cost_estimate=pl.CostEstimate(
            flops=2 * tokens * features * (units + columns),
            bytes_accessed=2 * features * (units + columns), transcendentals=0),
    )(hidden[0], down_weight[0], residual[0],
      norm_gain[0].reshape(n, 1, chunk), qkv_weight[0].reshape(n, chunk, columns))
    return (received[None], projected[None])


def solution(mesh):
    placed = (
        P("section", "groups", "tensor"),
        P("section", "tensor", None),
        P("section", "groups", "tensor"),
        P("section", None),
        P("section", None, "tensor"),
    )
    return jax.shard_map(
        functools.partial(body, mesh.shape["tensor"], mesh.shape["section"]),
        mesh=mesh,
        in_specs=placed,
        out_specs=(P("section", "groups", "tensor"), P("section", "groups", "tensor")),
        check_vma=False,
    )
```

```python
import functools

import jax
import jax.numpy as jnp
from jax import lax
from jax.experimental import pallas as pl
from jax.experimental.pallas import tpu as pltpu
from jax.sharding import PartitionSpec as P

epsilon = 1e-05
MESH = pl.DeviceIdType.MESH
PIECES = 4
BUFFERS = 4


def ring_order(n):
    inner = 1
    while inner * inner * 4 <= n:
        inner *= 2
    outer = n // inner
    if outer * inner != n or inner < 2 or outer % 2:
        return list(range(n))
    order = []
    for a in range(outer):
        columns = range(1, inner) if a % 2 == 0 else range(inner - 1, 0, -1)
        order += [a * inner + b for b in columns]
    return order + [a * inner for a in range(outer - 1, -1, -1)]


def lookup(table, index):
    found = jnp.int32(table[0])
    for k in range(1, len(table)):
        found = jnp.where(index == k, jnp.int32(table[k]), found)
    return found


def kernel(n, sections, hidden_far, down, residual_far, gain, qkv, received, projected,
           hidden, residual, w_buf, q_buf, part, rs, ag, acc, square, w_sem, q_sem, in_sem, rs_send, rs_recv,
           ag_send, ag_recv, swap_send, swap_recv):
    order = ring_order(n)
    position = [order.index(k) for k in range(n)]
    half, chunk = part.shape[2:]
    width = w_buf.shape[2]
    tiles = chunk // width
    rows = half // PIECES
    total_tiles = n * 2 * tiles

    me = lax.axis_index("tensor")
    here = lookup(position, me)
    at = lambda p: lookup(order, lax.rem(p + 2 * n, n))
    right, left = at(here + 1), at(here - 1)
    section = lax.axis_index("section")
    after = lax.rem(section + 1, sections)
    before = lax.rem(section + sections - 1, sections)
    towards = (right, left)

    def owner(s, d):
        return at(here - s) if d == 0 else at(here + s)

    def fetch(t):
        s = lax.div(t, 2 * tiles)
        d = lax.rem(lax.div(t, tiles), 2)
        j = lax.rem(t, tiles)
        c = at(here + (2 * d - 1) * (s + 1))
        start = pl.multiple_of(c * chunk + j * width, width)
        b = lax.rem(t, BUFFERS)
        return pltpu.make_async_copy(down.at[:, pl.ds(start, width)], w_buf.at[b], w_sem.at[b])

    hidden_copy = pltpu.make_async_copy(hidden_far, hidden, in_sem.at[0])
    residual_copy = pltpu.make_async_copy(residual_far, residual, in_sem.at[1])
    hidden_copy.start()
    for t in range(min(BUFFERS, total_tiles)):
        fetch(jnp.int32(t)).start()

    barrier = pltpu.get_barrier_semaphore()
    pl.semaphore_signal(barrier, inc=1, device_id={"tensor": left}, device_id_type=MESH)
    pl.semaphore_signal(barrier, inc=1, device_id={"tensor": right}, device_id_type=MESH)
    pl.semaphore_signal(barrier, inc=1, device_id={"section": before}, device_id_type=MESH)
    pl.semaphore_wait(barrier, 3)

    def span(piece):
        return pl.ds(piece * rows, rows)

    def rs_copy(s, d, piece):
        return pltpu.make_async_remote_copy(
            src_ref=rs.at[s, d, span(piece)],
            dst_ref=rs.at[s + 1, d, span(piece)],
            send_sem=rs_send.at[d, piece, lax.rem(s, 2)],
            recv_sem=rs_recv.at[d, piece, s],
            device_id={"tensor": towards[d]}, device_id_type=MESH)

    def swap_copy(d, piece):
        return pltpu.make_async_remote_copy(
            src_ref=rs.at[n - 1, d, span(piece)],
            dst_ref=ag.at[me, d, span(piece)],
            send_sem=swap_send.at[d, piece],
            recv_sem=swap_recv.at[d, piece],
            device_id={"section": after}, device_id_type=MESH)

    def ag_copy(s, d, piece, slot):
        return pltpu.make_async_remote_copy(
            src_ref=ag.at[slot, d, span(piece)],
            dst_ref=ag.at[slot, d, span(piece)],
            send_sem=ag_send.at[d, piece, lax.rem(s, 2)],
            recv_sem=ag_recv.at[d, piece, s],
            device_id={"tensor": towards[d]}, device_id_type=MESH)

    def multiply_some(s, first, last):
        def one(i, carry):
            d = lax.div(i, tiles)
            j = lax.rem(i, tiles)
            t = s * 2 * tiles + i
            fetch(t).wait()
            part[lax.rem(s, 2), d, :, pl.ds(pl.multiple_of(j * width, width), width)] = jnp.dot(
                hidden[pl.ds(pl.multiple_of(d * half, half), half), :], w_buf[lax.rem(t, BUFFERS)],
                preferred_element_type=jnp.float32)

            @pl.when(t + BUFFERS < total_tiles)
            def _():
                fetch(t + BUFFERS).start()
            return carry
        lax.fori_loop(first, last, one, 0)

    def combine(s, d, piece, first, last):
        value = part[lax.rem(s, 2), d, span(piece), :]
        if not first:
            rs_copy(s - 1, d, piece).wait_recv()
            value = value + rs[s, d, span(piece), :].astype(jnp.float32)
        if last:
            value = value + residual[pl.ds(d * half + piece * rows, rows), :].astype(jnp.float32)
        rs[s, d, span(piece), :] = value.astype(jnp.bfloat16)
        if last:
            swap_copy(d, piece).start()
        else:
            @pl.when(s >= 2)
            def _():
                rs_copy(s - 2, d, piece).wait_send()
            rs_copy(s, d, piece).start()

    zero = jnp.int32(0)
    hidden_copy.wait()
    for d in range(2):
        multiply_some(zero, d * tiles, (d + 1) * tiles)
        for piece in range(PIECES):
            combine(zero, d, piece, True, False)
    q_copy = pltpu.make_async_copy(qkv, q_buf, q_sem)
    q_copy.start()
    residual_copy.start()
    multiply_some(zero + 1, 0, 2 * tiles)

    def middle(s, carry):
        for piece in range(PIECES):
            for d in range(2):
                combine(s, d, piece, False, False)
            multiply_some(s + 1, 2 * tiles * piece // PIECES, 2 * tiles * (piece + 1) // PIECES)
        return carry
    lax.fori_loop(1, n - 1, middle, 0)

    def begin_gather(piece):
        for d in range(2):
            swap_copy(d, piece).wait_recv()
            ag_copy(zero, d, piece, me).start()

    residual_copy.wait()
    for piece in range(PIECES):
        for d in range(2):
            combine(zero + n - 1, d, piece, False, True)
        if piece:
            begin_gather(piece - 1)
    begin_gather(PIECES - 1)
    q_copy.wait()

    def project(d, c, first):
        x = ag[c, d].astype(jnp.float32)
        own = jnp.sum(x * x, axis=1, keepdims=True)
        scaled = (x * gain[c]).astype(jnp.bfloat16)
        product = jnp.dot(scaled, q_buf[c], preferred_element_type=jnp.float32)
        if first:
            square[d] = own
            acc[d] = product
        else:
            square[d] += own
            acc[d] += product

    own_copies = [pltpu.make_async_copy(ag.at[me, d], received.at[pl.ds(d * half, half)], in_sem.at[d])
                  for d in range(2)]
    for d in range(2):
        own_copies[d].start()
        project(d, me, True)

    def gather_step(s, first, last):
        for piece in range(PIECES):
            for d in range(2):
                slot = owner(s + 1, d)
                ag_copy(s, d, piece, slot).wait_recv()
                if not last:
                    if not first:
                        ag_copy(s - 1, d, piece, owner(s - 1, d)).wait_send()
                    ag_copy(s + 1, d, piece, slot).start()
            if not first and piece in (0, PIECES // 2):
                project(min(piece, 1), owner(s, min(piece, 1)), False)

    gather_step(zero, True, False)

    def gather(s, carry):
        gather_step(s, False, False)
        return carry
    lax.fori_loop(1, n - 2, gather, 0)
    gather_step(zero + n - 2, False, True)
    for d in range(2):
        project(d, owner(n - 1, d), False)

    for d in range(2):
        own_copies[d].wait()
        scale = lax.rsqrt(square[d] / (n * chunk) + epsilon)
        projected[pl.ds(d * half, half), :] = (acc[d] * scale).astype(jnp.bfloat16)

    for piece in range(PIECES):
        for d in range(2):
            swap_copy(d, piece).wait_send()
            for s in range(max(n - 3, 0), n - 1):
                rs_copy(jnp.int32(s), d, piece).wait_send()
                ag_copy(jnp.int32(s), d, piece, owner(s, d)).wait_send()


def hand_on(received_in, projected_in, received, projected, sems):
    half = received_in.shape[0] // 2
    copies = []
    for k, (source, target) in enumerate(((received_in, received), (projected_in, projected))):
        for d in range(2):
            part = pl.ds(d * half, half)
            copies.append(pltpu.make_async_copy(source.at[part], target.at[part], sems.at[k, d]))
    for copy in copies:
        copy.start()
    for copy in copies:
        copy.wait()


def body(n, sections, hidden, down_weight, residual, norm_gain, qkv_weight):
    tokens, units = hidden.shape[1:]
    chunk = residual.shape[2]
    columns = qkv_weight.shape[2]
    half = tokens // 2
    width = 256 if chunk % 256 == 0 else chunk
    bf16, f32 = jnp.bfloat16, jnp.float32
    vmem = pl.BlockSpec(memory_space=pltpu.VMEM)
    far = pl.BlockSpec(memory_space=pl.ANY)
    dma = pltpu.SemaphoreType.DMA
    features = n * chunk
    received, projected = pl.pallas_call(
        functools.partial(kernel, n, sections),
        out_shape=(jax.ShapeDtypeStruct((tokens, chunk), bf16),
                   jax.ShapeDtypeStruct((tokens, columns), bf16)),
        in_specs=[far, far, far, vmem, far],
        out_specs=(far, vmem),
        scratch_shapes=[
            pltpu.VMEM((tokens, units), bf16),
            pltpu.VMEM((tokens, chunk), bf16),
            pltpu.VMEM((BUFFERS, units, width), bf16),
            pltpu.VMEM((n, chunk, columns), bf16),
            pltpu.VMEM((2, 2, half, chunk), f32),
            pltpu.VMEM((n, 2, half, chunk), bf16),
            pltpu.VMEM((n, 2, half, chunk), bf16),
            pltpu.VMEM((2, half, columns), f32),
            pltpu.VMEM((2, half, 1), f32),
            dma((BUFFERS,)), dma, dma((2,)),
            dma((2, PIECES, 2)), dma((2, PIECES, n)),
            dma((2, PIECES, 2)), dma((2, PIECES, n)),
            dma((2, PIECES)), dma((2, PIECES)),
        ],
        compiler_params=pltpu.CompilerParams(
            collective_id=0, has_side_effects=True, vmem_limit_bytes=60 * 2 ** 20),
        cost_estimate=pl.CostEstimate(
            flops=2 * tokens * features * (units + columns),
            bytes_accessed=2 * features * (units + columns), transcendentals=0),
    )(hidden[0], down_weight[0], residual[0],
      norm_gain[0].reshape(n, 1, chunk), qkv_weight[0].reshape(n, chunk, columns))
    received, projected = pl.pallas_call(
        hand_on,
        out_shape=(jax.ShapeDtypeStruct((tokens, chunk), bf16),
                   jax.ShapeDtypeStruct((tokens, columns), bf16)),
        in_specs=[vmem, vmem],
        out_specs=(far, far),
        scratch_shapes=[dma((2, 2))],
    )(received, projected)
    return (received[None], projected[None])


def solution(mesh):
    placed = (
        P("section", "groups", "tensor"),
        P("section", "tensor", None),
        P("section", "groups", "tensor"),
        P("section", None),
        P("section", None, "tensor"),
    )
    return jax.shard_map(
        functools.partial(body, mesh.shape["tensor"], mesh.shape["section"]),
        mesh=mesh,
        in_specs=placed,
        out_specs=(P("section", "groups", "tensor"), P("section", "groups", "tensor")),
        check_vma=False,
    )
```

```python
import functools

import jax
import jax.numpy as jnp
from jax import lax
from jax.experimental import pallas as pl
from jax.experimental.pallas import tpu as pltpu
from jax.sharding import PartitionSpec as P

epsilon = 1e-05
MESH = pl.DeviceIdType.MESH
PIECES = 2
BUFFERS = 4


def ring_order(n):
    inner = 1
    while inner * inner * 4 <= n:
        inner *= 2
    outer = n // inner
    if outer * inner != n or inner < 2 or outer % 2:
        return list(range(n))
    order = []
    for a in range(outer):
        columns = range(1, inner) if a % 2 == 0 else range(inner - 1, 0, -1)
        order += [a * inner + b for b in columns]
    return order + [a * inner for a in range(outer - 1, -1, -1)]


def lookup(table, index):
    found = jnp.int32(table[0])
    for k in range(1, len(table)):
        found = jnp.where(index == k, jnp.int32(table[k]), found)
    return found


def kernel(n, sections, hidden_far, down, residual_far, gain, qkv, received, projected,
           hidden, residual, w_buf, q_buf, part, rs, ag, acc, square, w_sem, q_sem, in_sem, rs_send, rs_recv,
           ag_send, ag_recv, swap_send, swap_recv):
    order = ring_order(n)
    position = [order.index(k) for k in range(n)]
    half, chunk = part.shape[2:]
    width = w_buf.shape[2]
    tiles = chunk // width
    rows = half // PIECES
    total_tiles = n * 2 * tiles

    me = lax.axis_index("tensor")
    here = lookup(position, me)
    at = lambda p: lookup(order, lax.rem(p + 2 * n, n))
    right, left = at(here + 1), at(here - 1)
    section = lax.axis_index("section")
    after = lax.rem(section + 1, sections)
    before = lax.rem(section + sections - 1, sections)
    towards = (right, left)

    def owner(s, d):
        return at(here - s) if d == 0 else at(here + s)

    def fetch(t):
        s = lax.div(t, 2 * tiles)
        d = lax.rem(lax.div(t, tiles), 2)
        j = lax.rem(t, tiles)
        c = at(here + (2 * d - 1) * (s + 1))
        start = pl.multiple_of(c * chunk + j * width, width)
        b = lax.rem(t, BUFFERS)
        return pltpu.make_async_copy(down.at[:, pl.ds(start, width)], w_buf.at[b], w_sem.at[b])

    hidden_copy = pltpu.make_async_copy(hidden_far, hidden, in_sem.at[0])
    residual_copy = pltpu.make_async_copy(residual_far, residual, in_sem.at[1])
    hidden_copy.start()
    for t in range(min(BUFFERS, total_tiles)):
        fetch(jnp.int32(t)).start()

    barrier = pltpu.get_barrier_semaphore()
    pl.semaphore_signal(barrier, inc=1, device_id={"tensor": left}, device_id_type=MESH)
    pl.semaphore_signal(barrier, inc=1, device_id={"tensor": right}, device_id_type=MESH)
    pl.semaphore_signal(barrier, inc=1, device_id={"section": before}, device_id_type=MESH)
    pl.semaphore_wait(barrier, 3)

    def span(piece):
        return pl.ds(piece * rows, rows)

    def rs_copy(s, d, piece):
        return pltpu.make_async_remote_copy(
            src_ref=rs.at[s, d, span(piece)],
            dst_ref=rs.at[s + 1, d, span(piece)],
            send_sem=rs_send.at[d, piece, lax.rem(s, 2)],
            recv_sem=rs_recv.at[d, piece, s],
            device_id={"tensor": towards[d]}, device_id_type=MESH)

    def swap_copy(d, piece):
        return pltpu.make_async_remote_copy(
            src_ref=rs.at[n - 1, d, span(piece)],
            dst_ref=ag.at[me, d, span(piece)],
            send_sem=swap_send.at[d, piece],
            recv_sem=swap_recv.at[d, piece],
            device_id={"section": after}, device_id_type=MESH)

    def ag_copy(s, d, piece, slot):
        return pltpu.make_async_remote_copy(
            src_ref=ag.at[slot, d, span(piece)],
            dst_ref=ag.at[slot, d, span(piece)],
            send_sem=ag_send.at[d, piece, lax.rem(s, 2)],
            recv_sem=ag_recv.at[d, piece, s],
            device_id={"tensor": towards[d]}, device_id_type=MESH)

    def multiply_some(s, first, last):
        def one(i, carry):
            d = lax.div(i, tiles)
            j = lax.rem(i, tiles)
            t = s * 2 * tiles + i
            fetch(t).wait()
            part[lax.rem(s, 2), d, :, pl.ds(pl.multiple_of(j * width, width), width)] = jnp.dot(
                hidden[pl.ds(pl.multiple_of(d * half, half), half), :], w_buf[lax.rem(t, BUFFERS)],
                preferred_element_type=jnp.float32)

            @pl.when(t + BUFFERS < total_tiles)
            def _():
                fetch(t + BUFFERS).start()
            return carry
        lax.fori_loop(first, last, one, 0)

    def combine(s, d, piece, first, last):
        value = part[lax.rem(s, 2), d, span(piece), :]
        if not first:
            rs_copy(s - 1, d, piece).wait_recv()
            value = value + rs[s, d, span(piece), :].astype(jnp.float32)
        if last:
            value = value + residual[pl.ds(d * half + piece * rows, rows), :].astype(jnp.float32)
        rs[s, d, span(piece), :] = value.astype(jnp.bfloat16)
        if last:
            swap_copy(d, piece).start()
        else:
            @pl.when(s >= 2)
            def _():
                rs_copy(s - 2, d, piece).wait_send()
            rs_copy(s, d, piece).start()

    zero = jnp.int32(0)
    hidden_copy.wait()
    for d in range(2):
        multiply_some(zero, d * tiles, (d + 1) * tiles)
        for piece in range(PIECES):
            combine(zero, d, piece, True, False)
    q_copy = pltpu.make_async_copy(qkv, q_buf, q_sem)
    q_copy.start()
    residual_copy.start()
    multiply_some(zero + 1, 0, 2 * tiles)

    def middle(s, carry):
        for piece in range(PIECES):
            for d in range(2):
                combine(s, d, piece, False, False)
            multiply_some(s + 1, 2 * tiles * piece // PIECES, 2 * tiles * (piece + 1) // PIECES)
        return carry
    lax.fori_loop(1, n - 1, middle, 0)

    def begin_gather(piece):
        for d in range(2):
            swap_copy(d, piece).wait_recv()
            ag_copy(zero, d, piece, me).start()

    residual_copy.wait()
    for piece in range(PIECES):
        for d in range(2):
            combine(zero + n - 1, d, piece, False, True)
        if piece:
            begin_gather(piece - 1)
    begin_gather(PIECES - 1)
    q_copy.wait()

    def project(d, c, first):
        x = ag[c, d].astype(jnp.float32)
        own = jnp.sum(x * x, axis=1, keepdims=True)
        scaled = (x * gain[c]).astype(jnp.bfloat16)
        product = jnp.dot(scaled, q_buf[c], preferred_element_type=jnp.float32)
        if first:
            square[d] = own
            acc[d] = product
        else:
            square[d] += own
            acc[d] += product

    own_copies = [pltpu.make_async_copy(ag.at[me, d], received.at[pl.ds(d * half, half)], in_sem.at[d])
                  for d in range(2)]
    for d in range(2):
        own_copies[d].start()
        project(d, me, True)

    def gather_step(s, first, last):
        for piece in range(PIECES):
            for d in range(2):
                slot = owner(s + 1, d)
                ag_copy(s, d, piece, slot).wait_recv()
                if not last:
                    if not first:
                        ag_copy(s - 1, d, piece, owner(s - 1, d)).wait_send()
                    ag_copy(s + 1, d, piece, slot).start()
            if not first and piece in (0, PIECES // 2):
                project(min(piece, 1), owner(s, min(piece, 1)), False)

    gather_step(zero, True, False)

    def gather(s, carry):
        gather_step(s, False, False)
        return carry
    lax.fori_loop(1, n - 2, gather, 0)
    gather_step(zero + n - 2, False, True)
    for d in range(2):
        project(d, owner(n - 1, d), False)

    for d in range(2):
        own_copies[d].wait()
        scale = lax.rsqrt(square[d] / (n * chunk) + epsilon)
        projected[pl.ds(d * half, half), :] = (acc[d] * scale).astype(jnp.bfloat16)

    for piece in range(PIECES):
        for d in range(2):
            swap_copy(d, piece).wait_send()
            for s in range(max(n - 3, 0), n - 1):
                rs_copy(jnp.int32(s), d, piece).wait_send()
                ag_copy(jnp.int32(s), d, piece, owner(s, d)).wait_send()


def hand_on(received_in, projected_in, received, projected, sems):
    half = received_in.shape[0] // 2
    copies = []
    for k, (source, target) in enumerate(((received_in, received), (projected_in, projected))):
        for d in range(2):
            part = pl.ds(d * half, half)
            copies.append(pltpu.make_async_copy(source.at[part], target.at[part], sems.at[k, d]))
    for copy in copies:
        copy.start()
    for copy in copies:
        copy.wait()


def body(n, sections, hidden, down_weight, residual, norm_gain, qkv_weight):
    tokens, units = hidden.shape[1:]
    chunk = residual.shape[2]
    columns = qkv_weight.shape[2]
    half = tokens // 2
    width = 256 if chunk % 256 == 0 else chunk
    bf16, f32 = jnp.bfloat16, jnp.float32
    vmem = pl.BlockSpec(memory_space=pltpu.VMEM)
    far = pl.BlockSpec(memory_space=pl.ANY)
    dma = pltpu.SemaphoreType.DMA
    features = n * chunk
    received, projected = pl.pallas_call(
        functools.partial(kernel, n, sections),
        out_shape=(jax.ShapeDtypeStruct((tokens, chunk), bf16),
                   jax.ShapeDtypeStruct((tokens, columns), bf16)),
        in_specs=[far, far, far, vmem, far],
        out_specs=(far, vmem),
        scratch_shapes=[
            pltpu.VMEM((tokens, units), bf16),
            pltpu.VMEM((tokens, chunk), bf16),
            pltpu.VMEM((BUFFERS, units, width), bf16),
            pltpu.VMEM((n, chunk, columns), bf16),
            pltpu.VMEM((2, 2, half, chunk), f32),
            pltpu.VMEM((n, 2, half, chunk), bf16),
            pltpu.VMEM((n, 2, half, chunk), bf16),
            pltpu.VMEM((2, half, columns), f32),
            pltpu.VMEM((2, half, 1), f32),
            dma((BUFFERS,)), dma, dma((2,)),
            dma((2, PIECES, 2)), dma((2, PIECES, n)),
            dma((2, PIECES, 2)), dma((2, PIECES, n)),
            dma((2, PIECES)), dma((2, PIECES)),
        ],
        compiler_params=pltpu.CompilerParams(
            collective_id=0, has_side_effects=True, vmem_limit_bytes=60 * 2 ** 20),
        cost_estimate=pl.CostEstimate(
            flops=2 * tokens * features * (units + columns),
            bytes_accessed=2 * features * (units + columns), transcendentals=0),
    )(hidden[0], down_weight[0], residual[0],
      norm_gain[0].reshape(n, 1, chunk), qkv_weight[0].reshape(n, chunk, columns))
    received, projected = pl.pallas_call(
        hand_on,
        out_shape=(jax.ShapeDtypeStruct((tokens, chunk), bf16),
                   jax.ShapeDtypeStruct((tokens, columns), bf16)),
        in_specs=[vmem, vmem],
        out_specs=(far, far),
        scratch_shapes=[dma((2, 2))],
    )(received, projected)
    return (received[None], projected[None])


def solution(mesh):
    placed = (
        P("section", "groups", "tensor"),
        P("section", "tensor", None),
        P("section", "groups", "tensor"),
        P("section", None),
        P("section", None, "tensor"),
    )
    return jax.shard_map(
        functools.partial(body, mesh.shape["tensor"], mesh.shape["section"]),
        mesh=mesh,
        in_specs=placed,
        out_specs=(P("section", "groups", "tensor"), P("section", "groups", "tensor")),
        check_vma=False,
    )
```
